32 devices in a mesh: grp: 2 (over y), az: 4 (over x, core), ax: 4 (over z).
Axes of the slice: x: 2, y: 2, z: 4, core: 2. Of those that a mesh axis runs over, the one named last changes fastest.
Arguments:
- populations: float32 [2, 27, 2, 128, 512], P('grp', None, None, 'az', 'ax'), may hold values from 0.4 to 1.6
- relax_rates: float32 [2, 27], replicated, may hold values from 1 to 1.7
- tile_offsets: int32 [4, 4], P('ax'), may hold values from 0 to 3, each once within a row
Outputs:
- populations_next: float32 [2, 27, 2, 128, 512], P('grp', None, None, 'az', 'ax')
The draws below stay inside these ranges and needn't reach their ends.
Inputs may be any that keep to these rules, and one draw needn't show every extreme that they name: `tile_offsets`: each row is a permutation of the 4 block offsets.
All inputs are finite; a program needn't handle non-finite values.
Results may differ from the reference program's by a relative error of at most 0.0003.
Values sent between devices are 32-bit elements; how exact they have to be, the bound alone decides.
A program may use at most 64 MiB of HBM per device.

```python
import jax
import jax.numpy as jnp
from jax import lax

RADIAL = 2
AXIAL = 128
SLOTS = 8
AROUND = 128
LENGTH = 512
N_AZ = 4
N_AX = 4


def block_scale(own_key, shape, pieces, low, largest):
    level, own = 1.0, jax.random.fold_in(own_key, 6)
    for position, parts in pieces:
        draws = jnp.exp(jax.random.uniform(jax.random.fold_in(own, position), (parts,), jnp.float32, low / len(pieces), largest / len(pieces)))
        level = level * jnp.repeat(draws, shape[position] // parts).reshape([-1 if axis == position else 1 for axis in range(len(shape))])
    return level


def setup_inputs(seed: int = 0) -> dict:
    key_of = jax.random.split(jax.random.key(seed), 4)
    return {
        "populations": jnp.clip(0.4 + 1.2 * jax.random.uniform(key_of[0], (2, 27, RADIAL, AROUND, LENGTH), jnp.float32) ** block_scale(key_of[0], (2, 27, RADIAL, AROUND, LENGTH), ((0, 2), (3, 4), (4, 4)), -0.2, 0.2), 0.4, 1.6),
        "relax_rates": jnp.clip(jax.random.uniform(key_of[1], (2, 27), jnp.float32, 1.0, 1.7), 1.0, 1.7),
        "tile_offsets": jax.vmap(lambda own: jax.random.permutation(own, N_AZ))(jax.random.split(key_of[2], N_AX)).reshape((N_AX, N_AZ)).astype(jnp.int32),
    }


exact_mode = lax.Precision.HIGHEST


def single_weight(value):
    return 2.0 / 3.0 if value == 0 else 1.0 / 6.0


def lattice_tables():
    speeds = [(radial, around, along) for radial in (-1, 0, 1) for around in (-1, 0, 1) for along in (-1, 0, 1)]
    weights = [single_weight(vector[0]) * single_weight(vector[1]) * single_weight(vector[2]) for vector in speeds]
    powers = [(first, second, third) for first in range(3) for second in range(3) for third in range(3)]
    moments = [[float(vector[0] ** power[0] * vector[1] ** power[1] * vector[2] ** power[2]) for vector in speeds] for power in powers]
    inverse_one = {-1: (0.0, -0.5, 0.5), 0: (1.0, 0.0, -1.0), 1: (0.0, 0.5, 0.5)}
    inverse = [[inverse_one[vector[0]][power[0]] * inverse_one[vector[1]][power[1]] * inverse_one[vector[2]][power[2]] for power in powers] for vector in speeds]
    return speeds, weights, moments, inverse


def operators(relax_rates):
    speeds, weights, moments, inverse = lattice_tables()
    keeping = [0.0 if index in (0, 1, 3, 9) else 1.0 for index in range(27)]
    left_table = jnp.asarray([[inverse[row][col] / weights[row] for col in range(27)] for row in range(27)], dtype=jnp.float32)
    right_table = jnp.asarray([[moments[row][col] * weights[col] for col in range(27)] for row in range(27)], dtype=jnp.float32)
    scaled = relax_rates.astype(jnp.float32) * jnp.asarray(keeping, dtype=jnp.float32)
    return jnp.einsum('im,gm,mj->gij', left_table, scaled, right_table, precision=exact_mode)


def equilibrium(state):
    speeds, weights, moments, inverse = lattice_tables()
    weight_table = jnp.asarray(weights, dtype=jnp.float32)
    drift_table = jnp.asarray([[float(speeds[row][col]) * weights[row] for col in range(3)] for row in range(27)], dtype=jnp.float32)
    speed_table = jnp.asarray([[float(speeds[row][col]) for col in range(3)] for row in range(27)], dtype=jnp.float32)
    density = jnp.einsum('i,i...->...', weight_table, state, precision=exact_mode)
    flow = jnp.einsum('ik,i...->k...', drift_table, state, precision=exact_mode) / density
    project = jnp.einsum('ik,k...->i...', speed_table, flow, precision=exact_mode)
    square = jnp.sum(flow * flow, axis=0)
    return density * (1.0 + 3.0 * project + 4.5 * project * project - 1.5 * square)


def relax(state, collision_matrix):
    return state - jnp.einsum('ij,j...->i...', collision_matrix, state - equilibrium(state), precision=exact_mode)


def stream(post, low_ghost, high_ghost):
    outgoing = []
    for index in range(27):
        radial_step = index // 9 - 1
        around_step = (index // 3) % 3 - 1
        along_step = index % 3 - 1
        moved = jnp.roll(post[index], (around_step, along_step), axis=(1, 2))
        if radial_step == 1:
            moved = jnp.concatenate([low_ghost[index - 18][None], moved[:-1]], axis=0)
        elif radial_step == -1:
            moved = jnp.concatenate([moved[1:], high_ghost[index][None]], axis=0)
        outgoing.append(moved)
    return jnp.stack(outgoing)


def bounced(post):
    return jnp.stack([post[26 - index, -1] for index in range(9)])


def mirrored(post):
    rows = []
    for index in range(18, 27):
        around_step = (index // 3) % 3 - 1
        along_step = index % 3 - 1
        rows.append(jnp.roll(post[index - 18, 0], (around_step, along_step), axis=(0, 1)))
    return jnp.stack(rows)


def route(values, tile_offsets, direction):
    shaped = values.reshape(9, N_AZ, N_AZ, SLOTS, N_AX, AXIAL)
    blocks = jnp.arange(N_AZ, dtype=jnp.int32)[:, None, None]
    source = jnp.remainder(blocks + direction * tile_offsets.astype(jnp.int32).T[None, :, :], N_AZ).astype(jnp.int32)
    full_index = jnp.broadcast_to(source[None, :, :, None, :, None], shaped.shape)
    picked = jnp.take_along_axis(shaped, full_index, axis=1)
    return picked.reshape(9, AROUND, LENGTH)


def reference(populations, relax_rates, tile_offsets):
    matrices = operators(relax_rates)
    rate_fine = relax_rates[0, 12]
    rate_core = relax_rates[1, 12]
    annulus_post = relax(populations[0], matrices[0])
    core_post = relax(populations[1], matrices[1])
    annulus_face = annulus_post[:, 0]
    annulus_balance = equilibrium(annulus_face)
    to_core = annulus_balance[0:9] + (2.0 * rate_fine / rate_core) * (annulus_face[0:9] - annulus_balance[0:9])
    core_face = core_post[:, -1]
    core_balance = equilibrium(core_face)
    to_annulus = core_balance[18:27] + (rate_core / (2.0 * rate_fine)) * (core_face[18:27] - core_balance[18:27])
    core_ghost = route(to_core, tile_offsets, -1)
    annulus_ghost = route(to_annulus, tile_offsets, 1)
    core_next = stream(core_post, mirrored(core_post), core_ghost)
    middle = stream(annulus_post, annulus_ghost, bounced(annulus_post))
    second = relax(middle, matrices[0])
    annulus_next = stream(second, annulus_ghost, bounced(second))
    return jnp.stack([annulus_next, core_next])
```

```python
import functools

import jax
import jax.numpy as jnp
from jax import lax
from jax.experimental import pallas as pl
from jax.experimental.pallas import tpu as pltpu
from jax.sharding import PartitionSpec as P

TILE = 8
COMBOS = ((0, 0), (1, 0), (0, 1), (-1, 1), (-1, 0))
FIXED = (0, 1, 3, 9)


def velocity(radial, around, along):
    return 9 * (radial + 1) + 3 * (around + 1) + (along + 1)


def triples():
    for stride in (9, 3, 1):
        for base in range(27):
            if base // stride % 3 == 0:
                yield base, base + stride, base + 2 * stride


def moments_of(state):
    x = list(state)
    for low, mid, high in triples():
        even = x[high] + x[low]
        x[low], x[mid], x[high] = even + 4.0 * x[mid], x[high] - x[low], even
    return x


def populations_of(scaled):
    x = list(scaled)
    for low, mid, high in triples():
        zero, one, two = x[low], x[mid], x[high]
        half = 0.5 * two
        x[mid] = -half if zero is None else zero - half
        x[high] = two if one is None else two + one
        x[low] = two if one is None else two - one
    return x


def flow_of(moment):
    density = moment[0]
    drift = (moment[9], moment[3], moment[1])
    inverse = 1.0 / density
    speed = tuple(j * inverse for j in drift)
    return density, drift, speed


def collide(state, rate):
    moment = moments_of(state)
    density, drift, speed = flow = flow_of(moment)
    square = [drift[d] * speed[d] for d in range(3)]
    scaled = []
    for index in range(27):
        if index in FIXED:
            scaled.append(None)
            continue
        power = (index // 9, index // 3 % 3, index % 3)
        odd = [d for d in range(3) if power[d] == 1]
        two = [d for d in range(3) if power[d] == 2]
        third = (1.0 / 3.0) ** len(two)
        if len(odd) == 0:
            total = functools.reduce(lambda a, b: a + b, [square[d] for d in two])
            balance = density * third + total * (3.0 * third)
        elif len(odd) == 1:
            balance = drift[odd[0]] * third
        elif len(odd) == 2:
            balance = drift[odd[0]] * speed[odd[1]] * third
        else:
            balance = None
        off = moment[index] if balance is None else moment[index] - balance
        scaled.append(off * rate[index])
    change = populations_of(scaled)
    return [g - c for g, c in zip(state, change)], flow


def scaled_rates(rates_ref, group):
    out = []
    for index in range(27):
        power = (index // 9, index // 3 % 3, index % 3)
        scale = 1.0
        for p in power:
            scale *= 0.25 if p == 0 else 0.5
        out.append(None if index in FIXED else rates_ref[group, index] * scale)
    return out


def kernel(
    count,
    length,
    pop_ref,
    rates_ref,
    offset_ref,
    out_ref,
    source,
    first,
    second,
    result,
    outward,
    tile_send,
    tile_recv,
    ghost,
    row_send,
    row_recv,
    col_send,
    col_recv,
    load_sem,
    store_sem,
    tile_send_sem,
    tile_recv_sem,
    edge_send_sem,
    edge_recv_sem,
):
    rows = source.shape[2]
    cells = source.shape[3]
    slots = rows // count
    tiles = rows // TILE
    group = lax.axis_index("grp")
    place = lax.axis_index("az")
    block = lax.axis_index("ax")
    annulus = group == 0
    face = group
    back = 1 - group

    loads = [
        pltpu.make_async_copy(pop_ref.at[0, :, r], source.at[:, r], load_sem.at[k])
        for k, r in enumerate((face, back))
    ]
    for copy in loads:
        copy.start()

    def device(around, along):
        return {
            "grp": group,
            "az": lax.rem(place + around + count, count),
            "ax": lax.rem(block + along + length, length),
        }

    def across(position):
        return {"grp": 1 - group, "az": position, "ax": block}

    barrier = pltpu.get_barrier_semaphore()
    sides = [(i, j) for i in (-1, 0, 1) for j in (-1, 0, 1) if (i, j) != (0, 0)]
    for i, j in sides:
        pl.semaphore_signal(barrier, 1, device_id=device(i, j), device_id_type=pl.DeviceIdType.MESH)
    for d in range(count):
        pl.semaphore_signal(barrier, 1, device_id=across(d), device_id_type=pl.DeviceIdType.MESH)

    direction = 1 - 2 * group
    partner = [
        lax.rem(place + direction * offset_ref[0, q] + count, count) for q in range(count)
    ]
    lane = lax.broadcasted_iota(jnp.int32, (TILE, cells), 1)

    def window(t, shift=0):
        return pl.ds(pl.multiple_of(t * TILE, TILE) + (TILE - shift), TILE)

    own_rate = scaled_rates(rates_ref, group)
    wide = jnp.full((TILE, cells), rates_ref[0, 12], jnp.float32) * 2.0
    core_wide = jnp.full((TILE, cells), rates_ref[1, 12], jnp.float32)
    ratio = jnp.where(annulus, wide, core_wide) / jnp.where(annulus, core_wide, wide)
    sign = jnp.where(annulus, -1.0, 1.0)

    def first_plane(r, outgoing):
        def body(t, carry):
            here = pl.ds(pl.multiple_of(t * TILE, TILE), TILE)
            post, (density, _, speed) = collide([source[i, r, here] for i in range(27)], own_rate)
            for i in range(27):
                first[i, r, window(t)] = post[i]
            if outgoing:
                rho = density * (1.0 / 216.0)
                base = 1.0 - 1.5 * (speed[0] * speed[0] + speed[1] * speed[1] + speed[2] * speed[2])
                radial = sign * speed[0]
                for k in range(9):
                    project = radial
                    if k // 3 != 1:
                        project = project + float(k // 3 - 1) * speed[1]
                    if k % 3 != 1:
                        project = project + float(k % 3 - 1) * speed[2]
                    balance = rho * (base + project * (3.0 + 4.5 * project))
                    value = jnp.where(annulus, post[k], post[18 + k])
                    value = balance + ratio * (value - balance)
                    if slots >= TILE:
                        part = slots // TILE
                        outward[t // part, k, pl.ds(lax.rem(t, part) * TILE, TILE)] = value
                    else:
                        for n in range(TILE // slots):
                            outward[t * (TILE // slots) + n, k] = value[n * slots : (n + 1) * slots]
            return carry

        lax.fori_loop(0, tiles, body, 0)

    def pack_rows(buffer, phase, combos):
        for c in combos:
            radial, r = COMBOS[c]
            for along in (-1, 0, 1):
                n = 3 * c + along + 1
                row_send[phase, 0, n : n + 1] = buffer[
                    velocity(radial, 1, along), r, TILE + rows - 1 : TILE + rows
                ]
                row_send[phase, 1, n : n + 1] = buffer[velocity(radial, -1, along), r, TILE : TILE + 1]

    def pack_columns(buffer, phase, combos, start):
        def body(t, carry):
            here = pl.ds(pl.multiple_of(t * TILE, TILE), TILE)
            for side, along in ((0, 1), (1, -1)):
                packed = jnp.zeros((TILE, cells), jnp.float32) if start else col_send[phase, side, here]
                for c in combos:
                    radial, r = COMBOS[c]
                    for around in (-1, 0, 1):
                        n = 3 * c + around + 1
                        value = buffer[velocity(radial, around, along), r, window(t)]
                        turn = n + 1 if along == 1 else n
                        value = value if turn == 0 else pltpu.roll(value, turn, 1)
                        packed = jnp.where(lane == n, value, packed)
                col_send[phase, side, here] = packed
            return carry

        lax.fori_loop(0, tiles, body, 0)

    def edge_copies(phase):
        top = pl.ds(0, TILE)
        inner = pl.ds(TILE, rows)
        bottom = pl.ds(rows - TILE, TILE)
        after = pl.ds(rows + TILE, TILE)
        plan = []
        for side, step in ((0, 1), (1, -1)):
            sent, landing = col_send.at[phase, side], col_recv.at[phase, side]
            plan.append((row_send.at[phase, side], row_recv.at[phase, side], (step, 0)))
            plan.append((sent, landing.at[inner], (0, step)))
            plan.append((sent.at[bottom], landing.at[top], (1, step)))
            plan.append((sent.at[top], landing.at[after], (-1, step)))
        return [
            pltpu.make_async_remote_copy(
                src_ref=src,
                dst_ref=dst,
                send_sem=edge_send_sem.at[phase, k],
                recv_sem=edge_recv_sem.at[phase, k],
                device_id=device(*step),
                device_id_type=pl.DeviceIdType.MESH,
            )
            for k, (src, dst, step) in enumerate(plan)
        ]

    def unpack_rows(buffer, phase, combos):
        for c in combos:
            radial, r = COMBOS[c]
            for along in (-1, 0, 1):
                n = 3 * c + along + 1
                buffer[velocity(radial, 1, along), r, TILE - 1 : TILE] = row_recv[phase, 0, n : n + 1]
                buffer[velocity(radial, -1, along), r, TILE + rows : TILE + rows + 1] = row_recv[
                    phase, 1, n : n + 1
                ]

    def moved(buffer, phase, radial, r, around, along, t, index):
        value = buffer[index, r, window(t, around)]
        if along == 0:
            return value
        n = 3 * COMBOS.index((radial, r)) + around + 1
        side = 0 if along == 1 else 1
        edge = col_recv[phase, side, window(t, around)]
        spot = 0 if along == 1 else cells - 1
        turn = (spot - n) % cells
        edge = edge if turn == 0 else pltpu.roll(edge, turn, 1)
        return jnp.where(lane == spot, edge, pltpu.roll(value, along % cells, 1))

    def streamed(buffer, phase, r, t, low):
        values = []
        for index in range(27):
            radial, around, along = index // 9 - 1, index // 3 % 3 - 1, index % 3 - 1
            if radial == 1 and r == 0:
                if low == "mirror":
                    value = moved(buffer, phase, -1, 0, around, along, t, index - 18)
                else:
                    value = ghost[index - 18, pl.ds(pl.multiple_of(t * TILE, TILE), TILE)]
            elif radial == -1 and r == 1:
                if low == "mirror":
                    value = ghost[index, pl.ds(pl.multiple_of(t * TILE, TILE), TILE)]
                else:
                    value = buffer[26 - index, 1, window(t)]
            else:
                value = moved(buffer, phase, radial, r - radial, around, along, t, index)
            values.append(value)
        return values

    def finish_plane(buffer, phase, r, low):
        def body(t, carry):
            here = pl.ds(pl.multiple_of(t * TILE, TILE), TILE)
            values = streamed(buffer, phase, r, t, low)
            for index in range(27):
                result[index, r, here] = values[index]
            return carry

        lax.fori_loop(0, tiles, body, 0)

    def store(r):
        return pltpu.make_async_copy(result.at[:, r], out_ref.at[0, :, r], store_sem.at[r])

    tile_copies = [
        pltpu.make_async_remote_copy(
            src_ref=tile_send.at[d],
            dst_ref=tile_recv.at[place],
            send_sem=tile_send_sem.at[d],
            recv_sem=tile_recv_sem.at[place],
            device_id=across(d),
            device_id_type=pl.DeviceIdType.MESH,
        )
        for d in range(count)
    ]

    loads[0].wait()
    first_plane(face, True)
    for d in range(count):
        chosen = jnp.int32(0)
        for q in range(1, count):
            chosen = jnp.where(partner[q] == d, q, chosen)
        tile_send[d] = outward[chosen]
        if d == 0:
            pl.semaphore_wait(barrier, len(sides) + count)
        tile_copies[d].start()

    loads[1].wait()
    first_plane(back, False)
    pack_rows(first, 0, range(5))
    pack_columns(first, 0, range(5), True)
    edges = edge_copies(0)
    for copy in edges:
        copy.start()
    for copy in edges:
        copy.wait_recv()
    unpack_rows(first, 0, range(5))

    def take_ghost():
        for s in range(count):
            pltpu.make_async_remote_copy(
                src_ref=tile_send.at[s],
                dst_ref=tile_recv.at[s],
                send_sem=tile_send_sem.at[s],
                recv_sem=tile_recv_sem.at[s],
                device_id=across(s),
                device_id_type=pl.DeviceIdType.MESH,
            ).wait_recv()
        for q in range(count):
            ghost[:, q * slots : (q + 1) * slots] = tile_recv[partner[q]]

    @pl.when(annulus)
    def _():
        def middle_plane(r):
            def body(t, carry):
                post, _ = collide(streamed(first, 0, r, t, "ghost"), own_rate)
                for i in range(27):
                    second[i, r, window(t)] = post[i]
                return carry

            lax.fori_loop(0, tiles, body, 0)

        middle_plane(1)
        pack_rows(second, 1, (2, 3))
        pack_columns(second, 1, (2, 3), True)
        take_ghost()
        middle_plane(0)
        pack_rows(second, 1, (0, 1))
        pack_columns(second, 1, (0, 1), False)
        later = edge_copies(1)
        for copy in later:
            copy.start()
        for copy in later:
            copy.wait_recv()
        unpack_rows(second, 1, range(4))
        for r in (0, 1):
            finish_plane(second, 1, r, "ghost")
            store(r).start()
        for copy in later:
            copy.wait_send()

    @pl.when(group == 1)
    def _():
        finish_plane(first, 0, 0, "mirror")
        store(0).start()
        take_ghost()
        finish_plane(first, 0, 1, "mirror")
        store(1).start()

    for copy in edges + tile_copies:
        copy.wait_send()
    for r in (0, 1):
        store(r).wait()


def local(count, length, populations, relax_rates, tile_offsets):
    _, speeds, radial, rows, cells = populations.shape
    slots = rows // count
    f32 = jnp.float32
    tall = rows + 2 * TILE
    return pl.pallas_call(
        functools.partial(kernel, count, length),
        out_shape=jax.ShapeDtypeStruct(populations.shape, f32),
        in_specs=[
            pl.BlockSpec(memory_space=pl.ANY),
            pl.BlockSpec(memory_space=pltpu.SMEM),
            pl.BlockSpec(memory_space=pltpu.SMEM),
        ],
        out_specs=pl.BlockSpec(memory_space=pl.ANY),
        scratch_shapes=[
            pltpu.VMEM((speeds, radial, rows, cells), f32),
            pltpu.VMEM((speeds, radial, tall, cells), f32),
            pltpu.VMEM((speeds, radial, tall, cells), f32),
            pltpu.VMEM((speeds, radial, rows, cells), f32),
            pltpu.VMEM((count, 9, slots, cells), f32),
            pltpu.VMEM((count, 9, slots, cells), f32),
            pltpu.VMEM((count, 9, slots, cells), f32),
            pltpu.VMEM((9, rows, cells), f32),
            pltpu.VMEM((2, 2, 16, cells), f32),
            pltpu.VMEM((2, 2, 16, cells), f32),
            pltpu.VMEM((2, 2, rows, cells), f32),
            pltpu.VMEM((2, 2, tall, cells), f32),
            pltpu.SemaphoreType.DMA((2,)),
            pltpu.SemaphoreType.DMA((2,)),
            pltpu.SemaphoreType.DMA((count,)),
            pltpu.SemaphoreType.DMA((count,)),
            pltpu.SemaphoreType.DMA((2, 8)),
            pltpu.SemaphoreType.DMA((2, 8)),
        ],
        compiler_params=pltpu.CompilerParams(
            collective_id=0, has_side_effects=True, vmem_limit_bytes=32 * 1024 * 1024
        ),
    )(populations, relax_rates, tile_offsets)


def solution(mesh):
    in_specs = (P("grp", None, None, "az", "ax"), P(), P("ax", None))
    out_specs = P("grp", None, None, "az", "ax")
    body = functools.partial(local, mesh.shape["az"], mesh.shape["ax"])
    return jax.shard_map(body, mesh=mesh, in_specs=in_specs, out_specs=out_specs, check_vma=False)
```

```python
import functools

import jax
import jax.numpy as jnp
from jax import lax
from jax.experimental import pallas as pl
from jax.experimental.pallas import tpu as pltpu
from jax.sharding import PartitionSpec as P

TILE = 8
COMBOS = ((0, 0), (1, 0), (0, 1), (-1, 1), (-1, 0))
FIXED = (0, 1, 3, 9)


def velocity(radial, around, along):
    return 9 * (radial + 1) + 3 * (around + 1) + (along + 1)


def triples():
    for stride in (9, 3, 1):
        for base in range(27):
            if base // stride % 3 == 0:
                yield base, base + stride, base + 2 * stride


def moments_of(state):
    x = list(state)
    for low, mid, high in triples():
        even = x[high] + x[low]
        x[low], x[mid], x[high] = even + 4.0 * x[mid], x[high] - x[low], even
    return x


def populations_of(scaled):
    x = list(scaled)
    for low, mid, high in triples():
        zero, one, two = x[low], x[mid], x[high]
        half = 0.5 * two
        x[mid] = -half if zero is None else zero - half
        x[high] = two if one is None else two + one
        x[low] = two if one is None else two - one
    return x


def flow_of(moment):
    density = moment[0]
    drift = (moment[9], moment[3], moment[1])
    inverse = 1.0 / density
    speed = tuple(j * inverse for j in drift)
    return density, drift, speed


def collide(state, rate):
    moment = moments_of(state)
    density, drift, speed = flow = flow_of(moment)
    square = [drift[d] * speed[d] for d in range(3)]
    scaled = []
    for index in range(27):
        if index in FIXED:
            scaled.append(None)
            continue
        power = (index // 9, index // 3 % 3, index % 3)
        odd = [d for d in range(3) if power[d] == 1]
        two = [d for d in range(3) if power[d] == 2]
        third = (1.0 / 3.0) ** len(two)
        if len(odd) == 0:
            total = functools.reduce(lambda a, b: a + b, [square[d] for d in two])
            balance = density * third + total * (3.0 * third)
        elif len(odd) == 1:
            balance = drift[odd[0]] * third
        elif len(odd) == 2:
            balance = drift[odd[0]] * speed[odd[1]] * third
        else:
            balance = None
        off = moment[index] if balance is None else moment[index] - balance
        scaled.append(off * rate[index])
    change = populations_of(scaled)
    return [g - c for g, c in zip(state, change)], flow


def scaled_rates(rates_ref, group):
    out = []
    for index in range(27):
        power = (index // 9, index // 3 % 3, index % 3)
        scale = 1.0
        for p in power:
            scale *= 0.25 if p == 0 else 0.5
        out.append(None if index in FIXED else rates_ref[group, index] * scale)
    return out


def kernel(
    count,
    length,
    pop_ref,
    rates_hbm,
    offset_hbm,
    out_ref,
    rates_ref,
    offset_ref,
    source,
    first,
    second,
    outward,
    tile_send,
    tile_recv,
    ghost,
    row_send,
    row_recv,
    col_send,
    col_recv,
    load_sem,
    tile_send_sem,
    tile_recv_sem,
    edge_send_sem,
    edge_recv_sem,
):
    rows = source.shape[2]
    cells = source.shape[3]
    slots = rows // count
    tiles = rows // TILE
    group = lax.axis_index("grp")
    place = lax.axis_index("az")
    block = lax.axis_index("ax")
    annulus = group == 0
    face = group
    back = 1 - group

    settings = [
        pltpu.make_async_copy(rates_hbm, rates_ref, load_sem.at[tiles + 1]),
        pltpu.make_async_copy(offset_hbm, offset_ref, load_sem.at[tiles + 2]),
    ]
    loads = []
    for t in range(tiles):
        here = pl.ds(t * TILE, TILE)
        loads.append(
            pltpu.make_async_copy(
                pop_ref.at[0, :, face, here], source.at[:, face, here], load_sem.at[t]
            )
        )
    rest = pltpu.make_async_copy(pop_ref.at[0, :, back], source.at[:, back], load_sem.at[tiles])
    for copy in settings + loads + [rest]:
        copy.start()

    def device(around, along):
        return {
            "grp": group,
            "az": lax.rem(place + around + count, count),
            "ax": lax.rem(block + along + length, length),
        }

    def across(position):
        return {"grp": 1 - group, "az": position, "ax": block}

    barrier = pltpu.get_barrier_semaphore()
    sides = [(i, j) for i in (-1, 0, 1) for j in (-1, 0, 1) if (i, j) != (0, 0)]
    for i, j in sides:
        pl.semaphore_signal(barrier, 1, device_id=device(i, j), device_id_type=pl.DeviceIdType.MESH)
    for d in range(count):
        pl.semaphore_signal(barrier, 1, device_id=across(d), device_id_type=pl.DeviceIdType.MESH)

    for copy in settings:
        copy.wait()
    direction = 1 - 2 * group
    partner = [
        lax.rem(place + direction * offset_ref[0, q] + count, count) for q in range(count)
    ]
    lane = lax.broadcasted_iota(jnp.int32, (TILE, cells), 1)

    def window(t, shift=0):
        return pl.ds(pl.multiple_of(t * TILE, TILE) + (TILE - shift), TILE)

    own_rate = scaled_rates(rates_ref, group)
    wide = jnp.full((TILE, cells), rates_ref[0, 12], jnp.float32) * 2.0
    core_wide = jnp.full((TILE, cells), rates_ref[1, 12], jnp.float32)
    ratio = jnp.where(annulus, wide, core_wide) / jnp.where(annulus, core_wide, wide)
    sign = jnp.where(annulus, -1.0, 1.0)

    def first_plane(r, outgoing):
        def body(t, carry):
            here = pl.ds(pl.multiple_of(t * TILE, TILE), TILE)
            if outgoing:
                pltpu.make_async_copy(
                    pop_ref.at[0, :, r, here], source.at[:, r, here], load_sem.at[t]
                ).wait()
            post, (density, _, speed) = collide([source[i, r, here] for i in range(27)], own_rate)
            for i in range(27):
                first[i, r, window(t)] = post[i]
            if outgoing:
                rho = density * (1.0 / 216.0)
                base = 1.0 - 1.5 * (speed[0] * speed[0] + speed[1] * speed[1] + speed[2] * speed[2])
                radial = sign * speed[0]
                for k in range(9):
                    project = radial
                    if k // 3 != 1:
                        project = project + float(k // 3 - 1) * speed[1]
                    if k % 3 != 1:
                        project = project + float(k % 3 - 1) * speed[2]
                    balance = rho * (base + project * (3.0 + 4.5 * project))
                    value = jnp.where(annulus, post[k], post[18 + k])
                    value = balance + ratio * (value - balance)
                    if slots >= TILE:
                        part = slots // TILE
                        outward[t // part, k, pl.ds(lax.rem(t, part) * TILE, TILE)] = value
                    else:
                        for n in range(TILE // slots):
                            outward[t * (TILE // slots) + n, k] = value[n * slots : (n + 1) * slots]
            return carry

        lax.fori_loop(0, tiles, body, 0)

    def pack_rows(buffer, phase, combos):
        for c in combos:
            radial, r = COMBOS[c]
            for along in (-1, 0, 1):
                n = 3 * c + along + 1
                row_send[phase, 0, n : n + 1] = buffer[
                    velocity(radial, 1, along), r, TILE + rows - 1 : TILE + rows
                ]
                row_send[phase, 1, n : n + 1] = buffer[velocity(radial, -1, along), r, TILE : TILE + 1]

    def pack_columns(buffer, phase, combos, start):
        def body(t, carry):
            here = pl.ds(pl.multiple_of(t * TILE, TILE), TILE)
            for side, along in ((0, 1), (1, -1)):
                packed = jnp.zeros((TILE, cells), jnp.float32) if start else col_send[phase, side, here]
                for c in combos:
                    radial, r = COMBOS[c]
                    for around in (-1, 0, 1):
                        n = 3 * c + around + 1
                        value = buffer[velocity(radial, around, along), r, window(t)]
                        turn = n + 1 if along == 1 else n
                        value = value if turn == 0 else pltpu.roll(value, turn, 1)
                        packed = jnp.where(lane == n, value, packed)
                col_send[phase, side, here] = packed
            return carry

        lax.fori_loop(0, tiles, body, 0)

    def edge_copies(phase):
        top = pl.ds(0, TILE)
        inner = pl.ds(TILE, rows)
        bottom = pl.ds(rows - TILE, TILE)
        after = pl.ds(rows + TILE, TILE)
        plan = []
        for side, step in ((0, 1), (1, -1)):
            sent, landing = col_send.at[phase, side], col_recv.at[phase, side]
            plan.append((row_send.at[phase, side], row_recv.at[phase, side], (step, 0)))
            plan.append((sent, landing.at[inner], (0, step)))
            plan.append((sent.at[bottom], landing.at[top], (1, step)))
            plan.append((sent.at[top], landing.at[after], (-1, step)))
        return [
            pltpu.make_async_remote_copy(
                src_ref=src,
                dst_ref=dst,
                send_sem=edge_send_sem.at[phase, k],
                recv_sem=edge_recv_sem.at[phase, k],
                device_id=device(*step),
                device_id_type=pl.DeviceIdType.MESH,
            )
            for k, (src, dst, step) in enumerate(plan)
        ]

    def unpack_rows(buffer, phase, combos):
        for c in combos:
            radial, r = COMBOS[c]
            for along in (-1, 0, 1):
                n = 3 * c + along + 1
                buffer[velocity(radial, 1, along), r, TILE - 1 : TILE] = row_recv[phase, 0, n : n + 1]
                buffer[velocity(radial, -1, along), r, TILE + rows : TILE + rows + 1] = row_recv[
                    phase, 1, n : n + 1
                ]

    def moved(buffer, phase, radial, r, around, along, t, index):
        value = buffer[index, r, window(t, around)]
        if along == 0:
            return value
        n = 3 * COMBOS.index((radial, r)) + around + 1
        side = 0 if along == 1 else 1
        edge = col_recv[phase, side, window(t, around)]
        spot = 0 if along == 1 else cells - 1
        turn = (spot - n) % cells
        edge = edge if turn == 0 else pltpu.roll(edge, turn, 1)
        return jnp.where(lane == spot, edge, pltpu.roll(value, along % cells, 1))

    def streamed(buffer, phase, r, t, low):
        values = []
        for index in range(27):
            radial, around, along = index // 9 - 1, index // 3 % 3 - 1, index % 3 - 1
            if radial == 1 and r == 0:
                if low == "mirror":
                    value = moved(buffer, phase, -1, 0, around, along, t, index - 18)
                else:
                    value = ghost[index - 18, pl.ds(pl.multiple_of(t * TILE, TILE), TILE)]
            elif radial == -1 and r == 1:
                if low == "mirror":
                    value = ghost[index, pl.ds(pl.multiple_of(t * TILE, TILE), TILE)]
                else:
                    value = buffer[26 - index, 1, window(t)]
            else:
                value = moved(buffer, phase, radial, r - radial, around, along, t, index)
            values.append(value)
        return values

    def finish_plane(buffer, phase, r, low):
        def body(t, carry):
            here = pl.ds(pl.multiple_of(t * TILE, TILE), TILE)
            values = streamed(buffer, phase, r, t, low)
            for index in range(27):
                out_ref[0, index, r, here] = values[index]
            return carry

        lax.fori_loop(0, tiles, body, 0)

    tile_copies = [
        pltpu.make_async_remote_copy(
            src_ref=tile_send.at[d],
            dst_ref=tile_recv.at[place],
            send_sem=tile_send_sem.at[d],
            recv_sem=tile_recv_sem.at[place],
            device_id=across(d),
            device_id_type=pl.DeviceIdType.MESH,
        )
        for d in range(count)
    ]

    first_plane(face, True)
    for d in range(count):
        chosen = jnp.int32(0)
        for q in range(1, count):
            chosen = jnp.where(partner[q] == d, q, chosen)
        tile_send[d] = outward[chosen]
        if d == 0:
            pl.semaphore_wait(barrier, len(sides) + count)
        tile_copies[d].start()

    rest.wait()
    first_plane(back, False)
    pack_rows(first, 0, range(5))
    pack_columns(first, 0, range(5), True)
    edges = edge_copies(0)
    for copy in edges:
        copy.start()
    for copy in edges:
        copy.wait_recv()
    unpack_rows(first, 0, range(5))

    def take_ghost():
        for s in range(count):
            pltpu.make_async_remote_copy(
                src_ref=tile_send.at[s],
                dst_ref=tile_recv.at[s],
                send_sem=tile_send_sem.at[s],
                recv_sem=tile_recv_sem.at[s],
                device_id=across(s),
                device_id_type=pl.DeviceIdType.MESH,
            ).wait_recv()
        for q in range(count):
            ghost[:, q * slots : (q + 1) * slots] = tile_recv[partner[q]]

    @pl.when(annulus)
    def _():
        def middle_plane(r):
            def body(t, carry):
                post, _ = collide(streamed(first, 0, r, t, "ghost"), own_rate)
                for i in range(27):
                    second[i, r, window(t)] = post[i]
                return carry

            lax.fori_loop(0, tiles, body, 0)

        middle_plane(1)
        pack_rows(second, 1, (2, 3))
        pack_columns(second, 1, (2, 3), True)
        take_ghost()
        middle_plane(0)
        pack_rows(second, 1, (0, 1))
        pack_columns(second, 1, (0, 1), False)
        later = edge_copies(1)
        for copy in later:
            copy.start()
        for copy in later:
            copy.wait_recv()
        unpack_rows(second, 1, range(4))
        for r in (0, 1):
            finish_plane(second, 1, r, "ghost")
        for copy in later:
            copy.wait_send()

    @pl.when(group == 1)
    def _():
        finish_plane(first, 0, 0, "mirror")
        take_ghost()
        finish_plane(first, 0, 1, "mirror")

    for copy in edges + tile_copies:
        copy.wait_send()


def local(count, length, populations, relax_rates, tile_offsets):
    _, speeds, radial, rows, cells = populations.shape
    slots = rows // count
    f32 = jnp.float32
    tall = rows + 2 * TILE
    return pl.pallas_call(
        functools.partial(kernel, count, length),
        out_shape=jax.ShapeDtypeStruct(populations.shape, f32),
        in_specs=[
            pl.BlockSpec(memory_space=pltpu.HBM),
            pl.BlockSpec(memory_space=pltpu.HBM),
            pl.BlockSpec(memory_space=pltpu.HBM),
        ],
        out_specs=pl.BlockSpec(memory_space=pltpu.VMEM),
        scratch_shapes=[
            pltpu.SMEM(relax_rates.shape, f32),
            pltpu.SMEM(tile_offsets.shape, jnp.int32),
            pltpu.VMEM((speeds, radial, rows, cells), f32),
            pltpu.VMEM((speeds, radial, tall, cells), f32),
            pltpu.VMEM((speeds, radial, tall, cells), f32),
            pltpu.VMEM((count, 9, slots, cells), f32),
            pltpu.VMEM((count, 9, slots, cells), f32),
            pltpu.VMEM((count, 9, slots, cells), f32),
            pltpu.VMEM((9, rows, cells), f32),
            pltpu.VMEM((2, 2, 16, cells), f32),
            pltpu.VMEM((2, 2, 16, cells), f32),
            pltpu.VMEM((2, 2, rows, cells), f32),
            pltpu.VMEM((2, 2, tall, cells), f32),
            pltpu.SemaphoreType.DMA((rows // TILE + 3,)),
            pltpu.SemaphoreType.DMA((count,)),
            pltpu.SemaphoreType.DMA((count,)),
            pltpu.SemaphoreType.DMA((2, 8)),
            pltpu.SemaphoreType.DMA((2, 8)),
        ],
        compiler_params=pltpu.CompilerParams(
            collective_id=0, has_side_effects=True, vmem_limit_bytes=32 * 1024 * 1024
        ),
    )(*(pltpu.with_memory_space_constraint(x, pltpu.HBM) for x in (populations, relax_rates, tile_offsets)))


def solution(mesh):
    in_specs = (P("grp", None, None, "az", "ax"), P(), P("ax", None))
    out_specs = P("grp", None, None, "az", "ax")
    body = functools.partial(local, mesh.shape["az"], mesh.shape["ax"])
    return jax.shard_map(body, mesh=mesh, in_specs=in_specs, out_specs=out_specs, check_vma=False)
```

```python
import functools

import jax
import jax.numpy as jnp
from jax import lax
from jax.experimental import pallas as pl
from jax.experimental.pallas import tpu as pltpu
from jax.sharding import PartitionSpec as P

TILE = 8
COMBOS = ((0, 0), (1, 0), (0, 1), (-1, 1), (-1, 0))
FIXED = (0, 1, 3, 9)


def velocity(radial, around, along):
    return 9 * (radial + 1) + 3 * (around + 1) + (along + 1)


def triples():
    for stride in (9, 3, 1):
        for base in range(27):
            if base // stride % 3 == 0:
                yield base, base + stride, base + 2 * stride


def moments_of(state):
    x = list(state)
    for low, mid, high in triples():
        even = x[high] + x[low]
        x[low], x[mid], x[high] = even + 4.0 * x[mid], x[high] - x[low], even
    return x


def populations_of(scaled):
    x = list(scaled)
    for low, mid, high in triples():
        zero, one, two = x[low], x[mid], x[high]
        half = 0.5 * two
        x[mid] = -half if zero is None else zero - half
        x[high] = two if one is None else two + one
        x[low] = two if one is None else two - one
    return x


def flow_of(moment):
    density = moment[0]
    drift = (moment[9], moment[3], moment[1])
    inverse = 1.0 / density
    speed = tuple(j * inverse for j in drift)
    return density, drift, speed


def collide(state, rate):
    moment = moments_of(state)
    density, drift, speed = flow = flow_of(moment)
    square = [drift[d] * speed[d] for d in range(3)]
    scaled = []
    for index in range(27):
        if index in FIXED:
            scaled.append(None)
            continue
        power = (index // 9, index // 3 % 3, index % 3)
        odd = [d for d in range(3) if power[d] == 1]
        two = [d for d in range(3) if power[d] == 2]
        third = (1.0 / 3.0) ** len(two)
        if len(odd) == 0:
            total = functools.reduce(lambda a, b: a + b, [square[d] for d in two])
            balance = density * third + total * (3.0 * third)
        elif len(odd) == 1:
            balance = drift[odd[0]] * third
        elif len(odd) == 2:
            balance = drift[odd[0]] * speed[odd[1]] * third
        else:
            balance = None
        off = moment[index] if balance is None else moment[index] - balance
        scaled.append(off * rate[index])
    change = populations_of(scaled)
    return [g - c for g, c in zip(state, change)], flow


def scaled_rates(rates_ref, group):
    out = []
    for index in range(27):
        power = (index // 9, index // 3 % 3, index % 3)
        scale = 1.0
        for p in power:
            scale *= 0.25 if p == 0 else 0.5
        out.append(None if index in FIXED else rates_ref[group, index] * scale)
    return out


def streamer(ghost, col_recv):
    cells = ghost.shape[2]
    lane = lax.broadcasted_iota(jnp.int32, (TILE, cells), 1)

    def window(t, shift=0):
        return pl.ds(pl.multiple_of(t * TILE, TILE) + (TILE - shift), TILE)

    def moved(buffer, phase, radial, r, around, along, t, index):
        value = buffer[index, r, window(t, around)]
        if along == 0:
            return value
        n = 3 * COMBOS.index((radial, r)) + around + 1
        side = 0 if along == 1 else 1
        edge = col_recv[phase, side, window(t, around)]
        spot = 0 if along == 1 else cells - 1
        turn = (spot - n) % cells
        edge = edge if turn == 0 else pltpu.roll(edge, turn, 1)
        return jnp.where(lane == spot, edge, pltpu.roll(value, along % cells, 1))

    def streamed(buffer, phase, r, t, low):
        values = []
        for index in range(27):
            radial, around, along = index // 9 - 1, index // 3 % 3 - 1, index % 3 - 1
            if radial == 1 and r == 0:
                if low == "mirror":
                    value = moved(buffer, phase, -1, 0, around, along, t, index - 18)
                else:
                    value = ghost[index - 18, pl.ds(pl.multiple_of(t * TILE, TILE), TILE)]
            elif radial == -1 and r == 1:
                if low == "mirror":
                    value = ghost[index, pl.ds(pl.multiple_of(t * TILE, TILE), TILE)]
                else:
                    value = buffer[26 - index, 1, window(t)]
            else:
                value = moved(buffer, phase, radial, r - radial, around, along, t, index)
            values.append(value)
        return values

    return streamed


def final_kernel(first, second, ghost, col_recv, out_ref, result, store_sem):
    tiles = ghost.shape[1] // TILE
    streamed = streamer(ghost, col_recv)
    group = lax.axis_index("grp")

    def store(r, t):
        here = pl.ds(pl.multiple_of(t * TILE, TILE), TILE)
        return pltpu.make_async_copy(
            result.at[:, r, here], out_ref.at[0, :, r, here], store_sem.at[r, t]
        )

    def finish_planes(buffer, phase, low):
        for r in (0, 1):

            def body(t, carry):
                here = pl.ds(pl.multiple_of(t * TILE, TILE), TILE)
                values = streamed(buffer, phase, r, t, low)
                for index in range(27):
                    result[index, r, here] = values[index]
                store(r, t).start()
                return carry

            lax.fori_loop(0, tiles, body, 0)

    @pl.when(group == 0)
    def _():
        finish_planes(second, 1, "ghost")

    @pl.when(group == 1)
    def _():
        finish_planes(first, 0, "mirror")

    for r in (0, 1):
        for t in range(tiles):
            store(r, t).wait()


def kernel(
    count,
    length,
    pop_ref,
    rates_hbm,
    offset_hbm,
    first,
    second,
    ghost,
    col_recv,
    rates_ref,
    offset_ref,
    source,
    outward,
    tile_send,
    tile_recv,
    row_send,
    row_recv,
    col_send,
    load_sem,
    tile_send_sem,
    tile_recv_sem,
    edge_send_sem,
    edge_recv_sem,
):
    rows = source.shape[2]
    cells = source.shape[3]
    slots = rows // count
    tiles = rows // TILE
    group = lax.axis_index("grp")
    place = lax.axis_index("az")
    block = lax.axis_index("ax")
    annulus = group == 0
    face = group
    back = 1 - group

    settings = [
        pltpu.make_async_copy(rates_hbm, rates_ref, load_sem.at[tiles + 1]),
        pltpu.make_async_copy(offset_hbm, offset_ref, load_sem.at[tiles + 2]),
    ]
    loads = []
    for t in range(tiles):
        here = pl.ds(t * TILE, TILE)
        loads.append(
            pltpu.make_async_copy(
                pop_ref.at[0, :, face, here], source.at[:, face, here], load_sem.at[t]
            )
        )
    rest = pltpu.make_async_copy(pop_ref.at[0, :, back], source.at[:, back], load_sem.at[tiles])
    for copy in settings + loads + [rest]:
        copy.start()

    def wrapped(value, size):
        value = jnp.where(value < 0, value + size, value)
        return jnp.where(value >= size, value - size, value)

    near_az = {i: wrapped(place + i, count) if i else place for i in (-1, 0, 1)}
    near_ax = {j: wrapped(block + j, length) if j else block for j in (-1, 0, 1)}
    spread = [wrapped(place + i, count) if i else place for i in range(count)]

    def device(around, along):
        return {"grp": group, "az": near_az[around], "ax": near_ax[along]}

    def across(position):
        return {"grp": 1 - group, "az": position, "ax": block}

    barrier = pltpu.get_barrier_semaphore()
    sides = [(i, j) for i in (-1, 0, 1) for j in (-1, 0, 1) if (i, j) != (0, 0)]
    for i, j in sides:
        pl.semaphore_signal(barrier, 1, device_id=device(i, j), device_id_type=pl.DeviceIdType.MESH)
    for d in range(count):
        pl.semaphore_signal(barrier, 1, device_id=across(d), device_id_type=pl.DeviceIdType.MESH)

    for copy in settings:
        copy.wait()
    direction = 1 - 2 * group
    partner = [wrapped(place + direction * offset_ref[0, q], count) for q in range(count)]
    lane = lax.broadcasted_iota(jnp.int32, (TILE, cells), 1)

    def window(t, shift=0):
        return pl.ds(pl.multiple_of(t * TILE, TILE) + (TILE - shift), TILE)

    own_rate = scaled_rates(rates_ref, group)
    wide = jnp.full((TILE, cells), rates_ref[0, 12], jnp.float32) * 2.0
    core_wide = jnp.full((TILE, cells), rates_ref[1, 12], jnp.float32)
    ratio = jnp.where(annulus, wide, core_wide) / jnp.where(annulus, core_wide, wide)
    sign = jnp.where(annulus, -1.0, 1.0)

    def first_plane(r, outgoing):
        def body(t, carry):
            here = pl.ds(pl.multiple_of(t * TILE, TILE), TILE)
            if outgoing:
                pltpu.make_async_copy(
                    pop_ref.at[0, :, r, here], source.at[:, r, here], load_sem.at[t]
                ).wait()
            post, (density, _, speed) = collide([source[i, r, here] for i in range(27)], own_rate)
            for i in range(27):
                first[i, r, window(t)] = post[i]
            if outgoing:
                rho = density * (1.0 / 216.0)
                base = 1.0 - 1.5 * (speed[0] * speed[0] + speed[1] * speed[1] + speed[2] * speed[2])
                radial = sign * speed[0]
                for k in range(9):
                    project = radial
                    if k // 3 != 1:
                        project = project + float(k // 3 - 1) * speed[1]
                    if k % 3 != 1:
                        project = project + float(k % 3 - 1) * speed[2]
                    balance = rho * (base + project * (3.0 + 4.5 * project))
                    value = jnp.where(annulus, post[k], post[18 + k])
                    value = balance + ratio * (value - balance)
                    if slots >= TILE:
                        part = slots // TILE
                        outward[t // part, k, pl.ds(lax.rem(t, part) * TILE, TILE)] = value
                    else:
                        for n in range(TILE // slots):
                            outward[t * (TILE // slots) + n, k] = value[n * slots : (n + 1) * slots]
            return carry

        lax.fori_loop(0, tiles, body, 0)

    def pack_rows(buffer, phase, combos):
        for c in combos:
            radial, r = COMBOS[c]
            for along in (-1, 0, 1):
                n = 3 * c + along + 1
                row_send[phase, 0, n : n + 1] = buffer[
                    velocity(radial, 1, along), r, TILE + rows - 1 : TILE + rows
                ]
                row_send[phase, 1, n : n + 1] = buffer[velocity(radial, -1, along), r, TILE : TILE + 1]

    def pack_columns(buffer, phase, combos, start):
        def body(t, carry):
            here = pl.ds(pl.multiple_of(t * TILE, TILE), TILE)
            for side, along in ((0, 1), (1, -1)):
                packed = jnp.zeros((TILE, cells), jnp.float32) if start else col_send[phase, side, here]
                for c in combos:
                    radial, r = COMBOS[c]
                    for around in (-1, 0, 1):
                        n = 3 * c + around + 1
                        value = buffer[velocity(radial, around, along), r, window(t)]
                        turn = n + 1 if along == 1 else n
                        value = value if turn == 0 else pltpu.roll(value, turn, 1)
                        packed = jnp.where(lane == n, value, packed)
                col_send[phase, side, here] = packed
            return carry

        lax.fori_loop(0, tiles, body, 0)

    def edge_copies(phase):
        top = pl.ds(0, TILE)
        inner = pl.ds(TILE, rows)
        bottom = pl.ds(rows - TILE, TILE)
        after = pl.ds(rows + TILE, TILE)
        plan = []
        for side, step in ((0, 1), (1, -1)):
            sent, landing = col_send.at[phase, side], col_recv.at[phase, side]
            plan.append((row_send.at[phase, side], row_recv.at[phase, side], (step, 0)))
            plan.append((sent, landing.at[inner], (0, step)))
            plan.append((sent.at[bottom], landing.at[top], (1, step)))
            plan.append((sent.at[top], landing.at[after], (-1, step)))
        return [
            pltpu.make_async_remote_copy(
                src_ref=src,
                dst_ref=dst,
                send_sem=edge_send_sem.at[phase, k],
                recv_sem=edge_recv_sem.at[phase, k],
                device_id=device(*step),
                device_id_type=pl.DeviceIdType.MESH,
            )
            for k, (src, dst, step) in enumerate(plan)
        ]

    def unpack_rows(buffer, phase, combos):
        for c in combos:
            radial, r = COMBOS[c]
            for along in (-1, 0, 1):
                n = 3 * c + along + 1
                buffer[velocity(radial, 1, along), r, TILE - 1 : TILE] = row_recv[phase, 0, n : n + 1]
                buffer[velocity(radial, -1, along), r, TILE + rows : TILE + rows + 1] = row_recv[
                    phase, 1, n : n + 1
                ]

    streamed = streamer(ghost, col_recv)

    tile_copies = [
        pltpu.make_async_remote_copy(
            src_ref=tile_send.at[d],
            dst_ref=tile_recv.at[place],
            send_sem=tile_send_sem.at[d],
            recv_sem=tile_recv_sem.at[place],
            device_id=across(spread[d]),
            device_id_type=pl.DeviceIdType.MESH,
        )
        for d in range(count)
    ]

    first_plane(face, True)
    for d in range(count):
        chosen = jnp.int32(0)
        for q in range(1, count):
            chosen = jnp.where(partner[q] == spread[d], q, chosen)
        tile_send[d] = outward[chosen]
        if d == 0:
            pl.semaphore_wait(barrier, len(sides) + count)
        tile_copies[d].start()

    rest.wait()
    first_plane(back, False)
    pack_rows(first, 0, range(5))
    pack_columns(first, 0, range(5), True)
    edges = edge_copies(0)
    for copy in edges:
        copy.start()
    for copy in edges:
        copy.wait_recv()
    unpack_rows(first, 0, range(5))

    def take_ghost():
        for s in range(count):
            pltpu.make_async_remote_copy(
                src_ref=tile_send.at[s],
                dst_ref=tile_recv.at[s],
                send_sem=tile_send_sem.at[s],
                recv_sem=tile_recv_sem.at[s],
                device_id=across(s),
                device_id_type=pl.DeviceIdType.MESH,
            ).wait_recv()
        for q in range(count):
            ghost[:, q * slots : (q + 1) * slots] = tile_recv[partner[q]]

    @pl.when(annulus)
    def _():
        def middle_plane(r):
            def body(t, carry):
                post, _ = collide(streamed(first, 0, r, t, "ghost"), own_rate)
                for i in range(27):
                    second[i, r, window(t)] = post[i]
                return carry

            lax.fori_loop(0, tiles, body, 0)

        middle_plane(1)
        pack_rows(second, 1, (2, 3))
        pack_columns(second, 1, (2, 3), True)
        take_ghost()
        middle_plane(0)
        pack_rows(second, 1, (0, 1))
        pack_columns(second, 1, (0, 1), False)
        later = edge_copies(1)
        for copy in later:
            copy.start()
        for copy in later:
            copy.wait_recv()
        unpack_rows(second, 1, range(4))
        for copy in later:
            copy.wait_send()

    @pl.when(group == 1)
    def _():
        take_ghost()

    for copy in edges + tile_copies:
        copy.wait_send()


def local(count, length, populations, relax_rates, tile_offsets):
    _, speeds, radial, rows, cells = populations.shape
    slots = rows // count
    f32 = jnp.float32
    tall = rows + 2 * TILE
    vmem = pl.BlockSpec(memory_space=pltpu.VMEM)
    hbm = pl.BlockSpec(memory_space=pltpu.HBM)
    inputs = [
        pltpu.with_memory_space_constraint(x, pltpu.HBM)
        for x in (populations, relax_rates, tile_offsets)
    ]
    parts = pl.pallas_call(
        functools.partial(kernel, count, length),
        out_shape=[
            jax.ShapeDtypeStruct((speeds, radial, tall, cells), f32),
            jax.ShapeDtypeStruct((speeds, radial, tall, cells), f32),
            jax.ShapeDtypeStruct((9, rows, cells), f32),
            jax.ShapeDtypeStruct((2, 2, tall, cells), f32),
        ],
        in_specs=[hbm] * 3,
        out_specs=[vmem] * 4,
        scratch_shapes=[
            pltpu.SMEM(relax_rates.shape, f32),
            pltpu.SMEM(tile_offsets.shape, jnp.int32),
            pltpu.VMEM((speeds, radial, rows, cells), f32),
            pltpu.VMEM((count, 9, slots, cells), f32),
            pltpu.VMEM((count, 9, slots, cells), f32),
            pltpu.VMEM((count, 9, slots, cells), f32),
            pltpu.VMEM((2, 2, 16, cells), f32),
            pltpu.VMEM((2, 2, 16, cells), f32),
            pltpu.VMEM((2, 2, rows, cells), f32),
            pltpu.SemaphoreType.DMA((rows // TILE + 3,)),
            pltpu.SemaphoreType.DMA((count,)),
            pltpu.SemaphoreType.DMA((count,)),
            pltpu.SemaphoreType.DMA((2, 8)),
            pltpu.SemaphoreType.DMA((2, 8)),
        ],
        compiler_params=pltpu.CompilerParams(
            collective_id=0, has_side_effects=True, vmem_limit_bytes=12 * 1024 * 1024
        ),
    )(*inputs)
    return pl.pallas_call(
        final_kernel,
        out_shape=jax.ShapeDtypeStruct(populations.shape, f32),
        in_specs=[vmem] * 4,
        out_specs=hbm,
        scratch_shapes=[
            pltpu.VMEM((speeds, radial, rows, cells), f32),
            pltpu.SemaphoreType.DMA((radial, rows // TILE)),
        ],
        compiler_params=pltpu.CompilerParams(vmem_limit_bytes=16 * 1024 * 1024),
    )(*parts)


def solution(mesh):
    in_specs = (P("grp", None, None, "az", "ax"), P(), P("ax", None))
    out_specs = P("grp", None, None, "az", "ax")
    body = functools.partial(local, mesh.shape["az"], mesh.shape["ax"])
    return jax.shard_map(body, mesh=mesh, in_specs=in_specs, out_specs=out_specs, check_vma=False)
```

```python
import functools

import jax
import jax.numpy as jnp
from jax import lax
from jax.experimental import pallas as pl
from jax.experimental.pallas import tpu as pltpu
from jax.sharding import PartitionSpec as P

TILE = 8
COMBOS = ((0, 0), (1, 0), (0, 1), (-1, 1), (-1, 0))
FIXED = (0, 1, 3, 9)


def velocity(radial, around, along):
    return 9 * (radial + 1) + 3 * (around + 1) + (along + 1)


def triples():
    for stride in (9, 3, 1):
        for base in range(27):
            if base // stride % 3 == 0:
                yield base, base + stride, base + 2 * stride


def moments_of(state):
    x = list(state)
    for low, mid, high in triples():
        even = x[high] + x[low]
        x[low], x[mid], x[high] = even + 4.0 * x[mid], x[high] - x[low], even
    return x


def populations_of(scaled):
    x = list(scaled)
    for low, mid, high in triples():
        zero, one, two = x[low], x[mid], x[high]
        half = 0.5 * two
        x[mid] = -half if zero is None else zero - half
        x[high] = two if one is None else two + one
        x[low] = two if one is None else two - one
    return x


def flow_of(moment):
    density = moment[0]
    drift = (moment[9], moment[3], moment[1])
    inverse = 1.0 / density
    speed = tuple(j * inverse for j in drift)
    return density, drift, speed


def collide(state, rate):
    moment = moments_of(state)
    density, drift, speed = flow = flow_of(moment)
    square = [drift[d] * speed[d] for d in range(3)]
    scaled = []
    for index in range(27):
        if index in FIXED:
            scaled.append(None)
            continue
        power = (index // 9, index // 3 % 3, index % 3)
        odd = [d for d in range(3) if power[d] == 1]
        two = [d for d in range(3) if power[d] == 2]
        third = (1.0 / 3.0) ** len(two)
        if len(odd) == 0:
            total = functools.reduce(lambda a, b: a + b, [square[d] for d in two])
            balance = density * third + total * (3.0 * third)
        elif len(odd) == 1:
            balance = drift[odd[0]] * third
        elif len(odd) == 2:
            balance = drift[odd[0]] * speed[odd[1]] * third
        else:
            balance = None
        off = moment[index] if balance is None else moment[index] - balance
        scaled.append(off * rate[index])
    change = populations_of(scaled)
    return [g - c for g, c in zip(state, change)], flow


def scaled_rates(rates_ref, group):
    out = []
    for index in range(27):
        power = (index // 9, index // 3 % 3, index % 3)
        scale = 1.0
        for p in power:
            scale *= 0.25 if p == 0 else 0.5
        out.append(None if index in FIXED else rates_ref[group, index] * scale)
    return out


def streamer(ghost, col_recv):
    cells = ghost.shape[2]
    lane = lax.broadcasted_iota(jnp.int32, (TILE, cells), 1)

    def window(t, shift=0):
        return pl.ds(pl.multiple_of(t * TILE, TILE) + (TILE - shift), TILE)

    def moved(buffer, phase, radial, r, around, along, t, index):
        value = buffer[index, r, window(t, around)]
        if along == 0:
            return value
        n = 3 * COMBOS.index((radial, r)) + around + 1
        side = 0 if along == 1 else 1
        edge = col_recv[phase, side, window(t, around)]
        spot = 0 if along == 1 else cells - 1
        turn = (spot - n) % cells
        edge = edge if turn == 0 else pltpu.roll(edge, turn, 1)
        return jnp.where(lane == spot, edge, pltpu.roll(value, along % cells, 1))

    def streamed(buffer, phase, r, t, low):
        values = []
        for index in range(27):
            radial, around, along = index // 9 - 1, index // 3 % 3 - 1, index % 3 - 1
            if radial == 1 and r == 0:
                if low == "mirror":
                    value = moved(buffer, phase, -1, 0, around, along, t, index - 18)
                else:
                    value = ghost[index - 18, pl.ds(pl.multiple_of(t * TILE, TILE), TILE)]
            elif radial == -1 and r == 1:
                if low == "mirror":
                    value = ghost[index, pl.ds(pl.multiple_of(t * TILE, TILE), TILE)]
                else:
                    value = buffer[26 - index, 1, window(t)]
            else:
                value = moved(buffer, phase, radial, r - radial, around, along, t, index)
            values.append(value)
        return values

    return streamed


def final_kernel(first, second, ghost, col_recv, out_ref, result, store_sem):
    tiles = ghost.shape[1] // TILE
    streamed = streamer(ghost, col_recv)
    group = lax.axis_index("grp")

    def store(r, t):
        here = pl.ds(pl.multiple_of(t * TILE, TILE), TILE)
        return pltpu.make_async_copy(
            result.at[:, r, here], out_ref.at[0, :, r, here], store_sem.at[r, t]
        )

    def finish_planes(buffer, phase, low):
        for r in (0, 1):

            def body(t, carry):
                here = pl.ds(pl.multiple_of(t * TILE, TILE), TILE)
                values = streamed(buffer, phase, r, t, low)
                for index in range(27):
                    result[index, r, here] = values[index]
                store(r, t).start()
                return carry

            lax.fori_loop(0, tiles, body, 0, unroll=True)

    @pl.when(group == 0)
    def _():
        finish_planes(second, 1, "ghost")

    @pl.when(group == 1)
    def _():
        finish_planes(first, 0, "mirror")

    for r in (0, 1):
        for t in range(tiles):
            store(r, t).wait()


def kernel(
    count,
    length,
    pop_ref,
    rates_hbm,
    offset_hbm,
    first,
    second,
    ghost,
    col_recv,
    rates_ref,
    offset_ref,
    source,
    outward,
    tile_send,
    tile_recv,
    row_send,
    row_recv,
    col_send,
    load_sem,
    tile_send_sem,
    tile_recv_sem,
    edge_send_sem,
    edge_recv_sem,
):
    rows = source.shape[2]
    cells = source.shape[3]
    slots = rows // count
    tiles = rows // TILE
    group = lax.axis_index("grp")
    place = lax.axis_index("az")
    block = lax.axis_index("ax")
    annulus = group == 0
    face = group
    back = 1 - group

    settings = [
        pltpu.make_async_copy(rates_hbm, rates_ref, load_sem.at[tiles + 1]),
        pltpu.make_async_copy(offset_hbm, offset_ref, load_sem.at[tiles + 2]),
    ]
    loads = []
    for t in range(tiles):
        here = pl.ds(t * TILE, TILE)
        loads.append(
            pltpu.make_async_copy(
                pop_ref.at[0, :, face, here], source.at[:, face, here], load_sem.at[t]
            )
        )
    rest = pltpu.make_async_copy(pop_ref.at[0, :, back], source.at[:, back], load_sem.at[tiles])
    for copy in settings + loads + [rest]:
        copy.start()

    def wrapped(value, size):
        value = jnp.where(value < 0, value + size, value)
        return jnp.where(value >= size, value - size, value)

    near_az = {i: wrapped(place + i, count) if i else place for i in (-1, 0, 1)}
    near_ax = {j: wrapped(block + j, length) if j else block for j in (-1, 0, 1)}
    spread = [wrapped(place + i, count) if i else place for i in range(count)]

    def device(around, along):
        return {"grp": group, "az": near_az[around], "ax": near_ax[along]}

    def across(position):
        return {"grp": 1 - group, "az": position, "ax": block}

    barrier = pltpu.get_barrier_semaphore()
    sides = [(i, j) for i in (-1, 0, 1) for j in (-1, 0, 1) if (i, j) != (0, 0)]
    for i, j in sides:
        pl.semaphore_signal(barrier, 1, device_id=device(i, j), device_id_type=pl.DeviceIdType.MESH)
    for d in range(count):
        pl.semaphore_signal(barrier, 1, device_id=across(d), device_id_type=pl.DeviceIdType.MESH)

    for copy in settings:
        copy.wait()
    direction = 1 - 2 * group
    partner = [wrapped(place + direction * offset_ref[0, q], count) for q in range(count)]
    lane = lax.broadcasted_iota(jnp.int32, (TILE, cells), 1)

    def window(t, shift=0):
        return pl.ds(pl.multiple_of(t * TILE, TILE) + (TILE - shift), TILE)

    own_rate = scaled_rates(rates_ref, group)
    wide = jnp.full((TILE, cells), rates_ref[0, 12], jnp.float32) * 2.0
    core_wide = jnp.full((TILE, cells), rates_ref[1, 12], jnp.float32)
    ratio = jnp.where(annulus, wide, core_wide) / jnp.where(annulus, core_wide, wide)
    sign = jnp.where(annulus, -1.0, 1.0)

    def first_plane(r, outgoing):
        def body(t, carry):
            here = pl.ds(pl.multiple_of(t * TILE, TILE), TILE)
            if outgoing:
                pltpu.make_async_copy(
                    pop_ref.at[0, :, r, here], source.at[:, r, here], load_sem.at[t]
                ).wait()
            post, (density, _, speed) = collide([source[i, r, here] for i in range(27)], own_rate)
            for i in range(27):
                first[i, r, window(t)] = post[i]
            if outgoing:
                rho = density * (1.0 / 216.0)
                base = 1.0 - 1.5 * (speed[0] * speed[0] + speed[1] * speed[1] + speed[2] * speed[2])
                radial = sign * speed[0]
                for k in range(9):
                    project = radial
                    if k // 3 != 1:
                        project = project + float(k // 3 - 1) * speed[1]
                    if k % 3 != 1:
                        project = project + float(k % 3 - 1) * speed[2]
                    balance = rho * (base + project * (3.0 + 4.5 * project))
                    value = jnp.where(annulus, post[k], post[18 + k])
                    value = balance + ratio * (value - balance)
                    if slots >= TILE:
                        part = slots // TILE
                        outward[t // part, k, pl.ds(lax.rem(t, part) * TILE, TILE)] = value
                    else:
                        for n in range(TILE // slots):
                            outward[t * (TILE // slots) + n, k] = value[n * slots : (n + 1) * slots]
            return carry

        lax.fori_loop(0, tiles, body, 0, unroll=True)

    def pack_rows(buffer, phase, combos):
        for c in combos:
            radial, r = COMBOS[c]
            for along in (-1, 0, 1):
                n = 3 * c + along + 1
                row_send[phase, 0, n : n + 1] = buffer[
                    velocity(radial, 1, along), r, TILE + rows - 1 : TILE + rows
                ]
                row_send[phase, 1, n : n + 1] = buffer[velocity(radial, -1, along), r, TILE : TILE + 1]

    def pack_columns(buffer, phase, combos, start):
        def body(t, carry):
            here = pl.ds(pl.multiple_of(t * TILE, TILE), TILE)
            for side, along in ((0, 1), (1, -1)):
                packed = jnp.zeros((TILE, cells), jnp.float32) if start else col_send[phase, side, here]
                for c in combos:
                    radial, r = COMBOS[c]
                    for around in (-1, 0, 1):
                        n = 3 * c + around + 1
                        value = buffer[velocity(radial, around, along), r, window(t)]
                        turn = n + 1 if along == 1 else n
                        value = value if turn == 0 else pltpu.roll(value, turn, 1)
                        packed = jnp.where(lane == n, value, packed)
                col_send[phase, side, here] = packed
            return carry

        lax.fori_loop(0, tiles, body, 0, unroll=True)

    def edge_copies(phase):
        top = pl.ds(0, TILE)
        inner = pl.ds(TILE, rows)
        bottom = pl.ds(rows - TILE, TILE)
        after = pl.ds(rows + TILE, TILE)
        plan = []
        for side, step in ((0, 1), (1, -1)):
            sent, landing = col_send.at[phase, side], col_recv.at[phase, side]
            plan.append((row_send.at[phase, side], row_recv.at[phase, side], (step, 0)))
            plan.append((sent, landing.at[inner], (0, step)))
            plan.append((sent.at[bottom], landing.at[top], (1, step)))
            plan.append((sent.at[top], landing.at[after], (-1, step)))
        return [
            pltpu.make_async_remote_copy(
                src_ref=src,
                dst_ref=dst,
                send_sem=edge_send_sem.at[phase, k],
                recv_sem=edge_recv_sem.at[phase, k],
                device_id=device(*step),
                device_id_type=pl.DeviceIdType.MESH,
            )
            for k, (src, dst, step) in enumerate(plan)
        ]

    def unpack_rows(buffer, phase, combos):
        for c in combos:
            radial, r = COMBOS[c]
            for along in (-1, 0, 1):
                n = 3 * c + along + 1
                buffer[velocity(radial, 1, along), r, TILE - 1 : TILE] = row_recv[phase, 0, n : n + 1]
                buffer[velocity(radial, -1, along), r, TILE + rows : TILE + rows + 1] = row_recv[
                    phase, 1, n : n + 1
                ]

    streamed = streamer(ghost, col_recv)

    tile_copies = [
        pltpu.make_async_remote_copy(
            src_ref=tile_send.at[d],
            dst_ref=tile_recv.at[place],
            send_sem=tile_send_sem.at[d],
            recv_sem=tile_recv_sem.at[place],
            device_id=across(spread[d]),
            device_id_type=pl.DeviceIdType.MESH,
        )
        for d in range(count)
    ]

    first_plane(face, True)
    for d in range(count):
        chosen = jnp.int32(0)
        for q in range(1, count):
            chosen = jnp.where(partner[q] == spread[d], q, chosen)
        tile_send[d] = outward[chosen]
        if d == 0:
            pl.semaphore_wait(barrier, len(sides) + count)
        tile_copies[d].start()

    rest.wait()
    first_plane(back, False)
    pack_rows(first, 0, range(5))
    pack_columns(first, 0, range(5), True)
    edges = edge_copies(0)
    for copy in edges:
        copy.start()
    for copy in edges:
        copy.wait_recv()
    unpack_rows(first, 0, range(5))

    def take_ghost():
        for s in range(count):
            pltpu.make_async_remote_copy(
                src_ref=tile_send.at[s],
                dst_ref=tile_recv.at[s],
                send_sem=tile_send_sem.at[s],
                recv_sem=tile_recv_sem.at[s],
                device_id=across(s),
                device_id_type=pl.DeviceIdType.MESH,
            ).wait_recv()
        for q in range(count):
            ghost[:, q * slots : (q + 1) * slots] = tile_recv[partner[q]]

    @pl.when(annulus)
    def _():
        def middle_plane(r):
            def body(t, carry):
                post, _ = collide(streamed(first, 0, r, t, "ghost"), own_rate)
                for i in range(27):
                    second[i, r, window(t)] = post[i]
                return carry

            lax.fori_loop(0, tiles, body, 0, unroll=True)

        middle_plane(1)
        pack_rows(second, 1, (2, 3))
        pack_columns(second, 1, (2, 3), True)
        take_ghost()
        middle_plane(0)
        pack_rows(second, 1, (0, 1))
        pack_columns(second, 1, (0, 1), False)
        later = edge_copies(1)
        for copy in later:
            copy.start()
        for copy in later:
            copy.wait_recv()
        unpack_rows(second, 1, range(4))
        for copy in later:
            copy.wait_send()

    @pl.when(group == 1)
    def _():
        take_ghost()

    for copy in edges + tile_copies:
        copy.wait_send()


def local(count, length, populations, relax_rates, tile_offsets):
    _, speeds, radial, rows, cells = populations.shape
    slots = rows // count
    f32 = jnp.float32
    tall = rows + 2 * TILE
    vmem = pl.BlockSpec(memory_space=pltpu.VMEM)
    hbm = pl.BlockSpec(memory_space=pltpu.HBM)
    inputs = [
        pltpu.with_memory_space_constraint(x, pltpu.HBM)
        for x in (populations, relax_rates, tile_offsets)
    ]
    parts = pl.pallas_call(
        functools.partial(kernel, count, length),
        out_shape=[
            jax.ShapeDtypeStruct((speeds, radial, tall, cells), f32),
            jax.ShapeDtypeStruct((speeds, radial, tall, cells), f32),
            jax.ShapeDtypeStruct((9, rows, cells), f32),
            jax.ShapeDtypeStruct((2, 2, tall, cells), f32),
        ],
        in_specs=[hbm] * 3,
        out_specs=[vmem] * 4,
        scratch_shapes=[
            pltpu.SMEM(relax_rates.shape, f32),
            pltpu.SMEM(tile_offsets.shape, jnp.int32),
            pltpu.VMEM((speeds, radial, rows, cells), f32),
            pltpu.VMEM((count, 9, slots, cells), f32),
            pltpu.VMEM((count, 9, slots, cells), f32),
            pltpu.VMEM((count, 9, slots, cells), f32),
            pltpu.VMEM((2, 2, 16, cells), f32),
            pltpu.VMEM((2, 2, 16, cells), f32),
            pltpu.VMEM((2, 2, rows, cells), f32),
            pltpu.SemaphoreType.DMA((rows // TILE + 3,)),
            pltpu.SemaphoreType.DMA((count,)),
            pltpu.SemaphoreType.DMA((count,)),
            pltpu.SemaphoreType.DMA((2, 8)),
            pltpu.SemaphoreType.DMA((2, 8)),
        ],
        compiler_params=pltpu.CompilerParams(
            collective_id=0, has_side_effects=True, vmem_limit_bytes=12 * 1024 * 1024
        ),
    )(*inputs)
    return pl.pallas_call(
        final_kernel,
        out_shape=jax.ShapeDtypeStruct(populations.shape, f32),
        in_specs=[vmem] * 4,
        out_specs=hbm,
        scratch_shapes=[
            pltpu.VMEM((speeds, radial, rows, cells), f32),
            pltpu.SemaphoreType.DMA((radial, rows // TILE)),
        ],
        compiler_params=pltpu.CompilerParams(vmem_limit_bytes=16 * 1024 * 1024),
    )(*parts)


def solution(mesh):
    in_specs = (P("grp", None, None, "az", "ax"), P(), P("ax", None))
    out_specs = P("grp", None, None, "az", "ax")
    body = functools.partial(local, mesh.shape["az"], mesh.shape["ax"])
    return jax.shard_map(body, mesh=mesh, in_specs=in_specs, out_specs=out_specs, check_vma=False)
```
